32 devices in a mesh: groups: 2 (over y), gx: 4 (over z), gy: 2 (over x), col: 2 (over core).
Axes of the slice: x: 2, y: 2, z: 4, core: 2. Of those that a mesh axis runs over, the one named last changes fastest.
Arguments:
- factors: bfloat16 [8, 16, 64, 512], P(None, None, ('groups', 'gx'), ('gy', 'col')), parts along dimension 2, may hold values from -1 to 1
- coeffs: float32 [12, 8], P('groups'), parts along dimension 0, may hold values from -3 to 3
- diffusivity: float32 [16, 64, 512], P(None, ('groups', 'gx'), ('gy', 'col')), parts along dimension 1, may hold values from 0.5 to 1.5
- terminal: float32 [16, 64, 512], P(None, ('groups', 'gx'), ('gy', 'col')), parts along dimension 1, may hold values from -6 to 6
Outputs:
- adjoint: float32 [16, 64, 512], P(None, ('groups', 'gx'), ('gy', 'col')), parts along dimension 1
- gradient: float32 [16, 64, 512], P(None, ('groups', 'gx'), ('gy', 'col')), parts along dimension 1
The draws below stay inside these ranges and needn't reach their ends.
There are 2 independent parts, one for each index of `groups`. The reference program is written for one: setup_inputs(seed, part) draws one part's arguments, and reference() takes and returns one part's arrays. A program takes and returns all parts, laid end to end along the dimension named above; each array names one. Nothing has to cross between parts.
All inputs are finite; a program needn't handle non-finite values.
Results may differ from the reference program's by a relative error of at most 0.0003.
Values may be sent and summed in bfloat16 or wider, within the bound.
A program may use at most 64 MiB of HBM per device.

```python
import math
import jax
import jax.numpy as jnp

NZ = 16
RANK = 8
STEPS = 6
NX = 32
NY = 512


def levels(stream_key, dims, cuts, least, high):
    gain, own = 1.0, jax.random.fold_in(stream_key, 6)
    for axis_at, shards_of in cuts:
        draws = jnp.exp(jax.random.uniform(jax.random.fold_in(own, axis_at), (shards_of,), jnp.float32, least / len(cuts), high / len(cuts)))
        gain = gain * jnp.repeat(draws, dims[axis_at] // shards_of).reshape([-1 if axis == axis_at else 1 for axis in range(len(dims))])
    return gain


def normal_values(rng, shape, scale, reach, pieces=(), held_as=jnp.bfloat16):
    level = levels(rng, shape, pieces, -0.22, 0.18) if pieces else 1.0
    entries = jax.random.normal(rng, shape, jnp.float32) * scale * level
    return jnp.minimum(jnp.maximum(entries, -reach), reach).astype(held_as)


def setup_inputs(seed: int = 0, part: int = 0) -> dict:
    key_of = jax.random.split(jax.random.key(seed), 5)
    own_keys = jax.random.split(jax.random.fold_in(key_of[4], part), 5)
    return {
        "factors": normal_values(own_keys[0], (RANK, NZ, NX, NY), 0.2, 1.0, ((2, 4), (3, 4))),
        "coeffs": normal_values(own_keys[1], (STEPS, RANK), 1.0, 3.0, (), jnp.float32),
        "diffusivity": jnp.clip(jnp.exp(math.log(1.5) - 1.0986123 * jax.random.uniform(own_keys[2], (NZ, NX, NY), jnp.float32) ** levels(own_keys[2], (NZ, NX, NY), ((1, 4), (2, 4)), -0.2, 0.2)), 0.5, 1.5),
        "terminal": normal_values(own_keys[3], (NZ, NX, NY), 1.0, 6.0, ((1, 4), (2, 4)), jnp.float32),
    }


step_dt = 0.05


def neighbours(padded):
    center = padded[..., 1:-1, 1:-1]
    others = [padded[..., :-2, 1:-1], padded[..., 2:, 1:-1], padded[..., 1:-1, :-2], padded[..., 1:-1, 2:], jnp.roll(center, 1, -3), jnp.roll(center, -1, -3)]
    return center, others


def operate(kappa_pad, field_pad):
    kappa_mid, kappa_side = neighbours(kappa_pad)
    field_mid, field_side = neighbours(field_pad)
    summed = jnp.zeros_like(field_mid)
    for kappa_near, field_near in zip(kappa_side, field_side):
        summed = summed + 0.5 * (kappa_mid + kappa_near) * (field_near - field_mid)
    return summed


def sensitivity(state_pad, field_pad):
    state_mid, state_side = neighbours(state_pad)
    field_mid, field_side = neighbours(field_pad)
    summed = jnp.zeros_like(field_mid)
    for state_near, field_near in zip(state_side, field_side):
        summed = summed + (state_near - state_mid) * (field_near - field_mid)
    return -0.5 * summed


def rebuild(factors, coeff_row):
    summed = coeff_row[0] * factors[0].astype(jnp.float32)
    for rank_index in range(1, factors.shape[0]):
        summed = summed + coeff_row[rank_index] * factors[rank_index].astype(jnp.float32)
    return summed


def pad_cells(field):
    return jnp.pad(field, ((0, 0), (1, 1), (1, 1)))


def reference(factors, coeffs, diffusivity, terminal):
    kappa_pad = pad_cells(diffusivity)
    adjoint = terminal
    gradient = jnp.zeros_like(terminal)
    for step in range(STEPS - 1, -1, -1):
        state = rebuild(factors, coeffs[step])
        state_pad = pad_cells(state)
        adjoint_pad = pad_cells(adjoint)
        gradient = gradient + step_dt * sensitivity(state_pad, adjoint_pad)
        adjoint = adjoint + step_dt * (operate(kappa_pad, adjoint_pad) + (1.0 - 3.0 * state * state) * adjoint)
    return adjoint, gradient
```

```python
import functools

import jax
import jax.numpy as jnp
from jax import lax
from jax.experimental import pallas as pl
from jax.experimental.pallas import tpu as pltpu
from jax.sharding import PartitionSpec as P

step_dt = 0.05
wide = 3

ways = ((-1, 0), (1, 0), (0, 1), (0, -1), (-1, 1), (1, -1), (-1, -1), (1, 1))
opposite = (1, 0, 3, 2, 5, 4, 7, 6)


def roll_lanes(x, shift):
    shift = shift % x.shape[-1]
    return x if shift == 0 else pltpu.roll(x, shift, x.ndim - 1)


def roll_rows(x, shift):
    return pltpu.roll(x, shift % x.shape[-2], x.ndim - 2)


def width_of(step, width):
    return max(1, width - 1 - step % width)


def stride_of(width):
    half = 1
    while half < width:
        half *= 2
    return 2 * half


def kernel(
    width, counts, factors, coeffs, kappa_in, terminal, adjoint_out, gradient_out,
    natural, row_send, row_recv, pack_send, pack_recv, send_sem, recv_sem,
):
    gx_count, gy_count, col_count = counts
    steps = coeffs.shape[0]
    ranks = factors.shape[0]
    rows = natural.shape[1] // 16
    rounds = steps // width
    group = lax.axis_index("groups")
    gx = lax.axis_index("gx")
    y = lax.axis_index("gy") * col_count + lax.axis_index("col")
    y_count = gy_count * col_count

    def inside(way):
        ok = None
        for at, move, count in ((gx, way[0], gx_count), (y, way[1], y_count)):
            if move == 0:
                continue
            here = at > 0 if move < 0 else at < count - 1
            ok = here if ok is None else jnp.logical_and(ok, here)
        return ok

    def device(way):
        far = y + way[1]
        return (group, gx + way[0], far // col_count, far % col_count)

    exists = [inside(way) for way in ways]

    barrier = pltpu.get_barrier_semaphore()
    total = jnp.int32(0)
    for m, way in enumerate(ways):
        @pl.when(exists[m])
        def _(way=way):
            pl.semaphore_signal(
                barrier, inc=1, device_id=device(way), device_id_type=pl.DeviceIdType.MESH
            )
        total = total + exists[m].astype(jnp.int32)

    for m in range(8):
        @pl.when(jnp.logical_not(exists[m]))
        def _(m=m):
            if m < 2:
                row_recv[m] = jnp.zeros(row_recv.shape[1:], jnp.float32)
            else:
                pack_recv[m - 2] = jnp.zeros(pack_recv.shape[1:], jnp.float32)

    spans = {}
    at = 0
    group_rows = []
    fields_of = [["kappa", "adjoint0"]]
    for r in range(rounds):
        fields_of.append([r * width + j for j in range(width)])
    for r in range(1, rounds):
        fields_of.append(["adjoint%d" % r])
    home = {}
    for g, names in enumerate(fields_of):
        start = at
        slot = 0
        for name in names:
            w = width_of(name, width) if isinstance(name, int) else width
            spans[name] = (at, w)
            home[name] = (g, slot)
            at += w
            slot += rows
        group_rows.append((start, at - start))

    lane = lax.broadcasted_iota(jnp.int32, (8, 128), 1)

    def copy(g, m):
        back = opposite[m]
        if m < 2:
            start, count = group_rows[g]
            source = row_send.at[m, pl.ds(start, count)]
            target = row_recv.at[back, pl.ds(start, count)]
        else:
            source = pack_send.at[g]
            target = pack_recv.at[back - 2, g]
        return pltpu.make_async_remote_copy(
            src_ref=source, dst_ref=target,
            send_sem=send_sem.at[g, m], recv_sem=recv_sem.at[g, back],
            device_id=device(ways[m]), device_id_type=pl.DeviceIdType.MESH,
        )

    def send(g, values):
        names = fields_of[g]
        stride = stride_of(spans[names[0]][1])
        slot_at = ((lane + stride // 2) % 128) // stride
        for half in range(2):
            packed = jnp.zeros((8, 128), jnp.float32)
            for name, value in zip(names, values):
                first, w = spans[name]
                row_send[0, first : first + w, half] = value[half][:w]
                row_send[1, first : first + w, half] = value[half][rows - w :]
                for x in range(rows):
                    slot = home[name][1] + x
                    moved = roll_lanes(value[half][x], slot * stride)
                    packed = jnp.where(slot_at == slot, moved, packed)
            pack_send[g, half] = packed
        for m in range(8):
            @pl.when(exists[m])
            def _(m=m):
                copy(g, m).start()

    def arrive(g):
        for m in range(8):
            @pl.when(exists[m])
            def _(m=m):
                back = opposite[m]
                if m < 2:
                    start, count = group_rows[g]
                    source = row_send.at[back, pl.ds(start, count)]
                    target = row_recv.at[m, pl.ds(start, count)]
                else:
                    source = pack_send.at[g]
                    target = pack_recv.at[m - 2, g]
                pltpu.make_async_remote_copy(
                    src_ref=source, dst_ref=target,
                    send_sem=send_sem.at[g, back], recv_sem=recv_sem.at[g, m],
                    device_id=device(ways[m]), device_id_type=pl.DeviceIdType.MESH,
                ).wait_recv()

    def padded(name, value):
        g, base = home[name]
        first, w = spans[name]
        stride = stride_of(spans[fields_of[g][0]][1])
        from_right = lane % stride < stride // 2
        center, halo = [], []
        for half in range(2):
            center.append(jnp.concatenate(
                [row_recv[0, first : first + w, half], value[half],
                 row_recv[1, first : first + w, half]], axis=0))
            own = jnp.where(from_right, pack_recv[0, g, half], pack_recv[1, g, half])
            parts = [(own, range(rows))]
            if w > 1:
                up = jnp.where(from_right, pack_recv[2, g, half], pack_recv[4, g, half])
                down = jnp.where(from_right, pack_recv[5, g, half], pack_recv[3, g, half])
                parts = [(up, range(rows - w + 1, rows)), *parts, (down, range(w - 1))]
            halo.append(jnp.stack(
                [roll_lanes(tile, -(base + x) * stride) for tile, at in parts for x in at]))
        return center, halo

    def load(ref):
        return [
            jnp.stack([ref[pl.ds(half * rows + x, 8, stride=2 * rows), :] for x in range(rows)])
            for half in range(2)
        ]

    def trim(x, extra):
        return x[extra : x.shape[0] - extra] if extra else x

    adjoint = load(terminal)
    kappa = [x * (0.5 * step_dt) for x in load(kappa_in)]
    pl.semaphore_wait(barrier, total)
    send(0, [kappa, adjoint])

    states = []
    factor = [factors[k].astype(jnp.float32) for k in range(ranks)]
    for r in range(rounds):
        for j in range(width):
            t = steps - 1 - (r * width + j)
            total_state = coeffs[t, 0] * factor[0]
            for k in range(1, ranks):
                total_state = total_state + coeffs[t, k] * factor[k]
            natural[r * width + j] = total_state.reshape(natural.shape[1:])
            states.append(load(natural.at[r * width + j]))
        send(1 + r, states[r * width : (r + 1) * width])

    last = lane == 127
    start_lane = lane == 0
    near = lane < 64
    lane_ok = jnp.logical_or(
        jnp.logical_and(near, exists[2]), jnp.logical_and(jnp.logical_not(near), exists[3]))

    def ahead(center, halo):
        c, h = roll_lanes(center, -1), roll_lanes(halo, -1)
        return jnp.where(last, h, c), jnp.where(last, c, h)

    def behind(center, halo):
        c, h = roll_lanes(center, 1), roll_lanes(halo, 1)
        return jnp.where(start_lane, h, c), jnp.where(start_lane, c, h)

    def masked(x, b):
        if b == 0:
            return x
        return jnp.concatenate(
            [jnp.where(exists[0], x[:b], 0.0), x[b : b + rows],
             jnp.where(exists[1], x[b + rows :], 0.0)], axis=0)

    arrive(0)
    kc, kh = padded("kappa", kappa)
    face_x = [[x[half][1:] + x[half][:-1] for half in range(2)] for x in (kc, kh)]
    face_y = []
    for half in range(2):
        c = trim(kc[half], 1)
        ca, ha = ahead(c, kh[half])
        face_y.append((c + ca, kh[half] + ha))
    face_z = [(x[0] + x[1], x[1] + roll_rows(x[0], -1)) for x in (kc, kh)]

    gradient = [jnp.zeros((rows, 8, 128), jnp.float32) for _ in range(2)]
    for r in range(rounds):
        if r:
            send(rounds + r, [adjoint])
            arrive(rounds + r)
        vc, vh = padded("adjoint%d" % r, adjoint)
        arrive(1 + r)
        for j in range(width):
            index = r * width + j
            a = width - j
            b = a - 1
            skip = width - a
            sc, sh = padded(index, states[index])
            sw = spans[index][1]
            new_c, new_h = [None, None], [None, None]
            for half in range(2):
                d = vc[half][1:] - vc[half][:-1]
                flux = trim(face_x[0][half], skip) * d
                new_c[half] = flux[1:] - flux[:-1]
                ds = trim(sc[half], sw - 1)
                product = (ds[1:] - ds[:-1]) * trim(d, b)
                gradient[half] = gradient[half] + (product[1:] + product[:-1])
                if b:
                    d = vh[half][1:] - vh[half][:-1]
                    flux = trim(face_x[1][half], skip) * d
                    new_h[half] = flux[1:] - flux[:-1]
            for half in range(2):
                c, h = trim(vc[half], 1), vh[half]
                ca, ha = ahead(c, h)
                dc, dh = ca - c, ha - h
                fc = trim(face_y[half][0], skip) * dc
                fh = trim(face_y[half][1], skip) * dh
                bc, bh = behind(fc, fh)
                new_c[half] = new_c[half] + (fc - bc)
                if b:
                    new_h[half] = new_h[half] + trim(fh - bh, 1)
                c, h = trim(sc[half], sw), trim(sh[half], sw - 1)
                ca, ha = ahead(c, h)
                pc = (ca - c) * trim(dc, b)
                ph = (ha - h) * trim(dh, b)
                bc, _ = behind(pc, ph)
                gradient[half] = gradient[half] + (pc + bc)
            for which, v, new, extra in ((0, vc, new_c, skip + 1), (1, vh, new_h, skip + 1)):
                if which and not b:
                    continue
                v0, v1 = trim(v[0], 1), trim(v[1], 1)
                inner, outer = v1 - v0, roll_rows(v0, -1) - v1
                fi = trim(face_z[which][0], extra) * inner
                fo = trim(face_z[which][1], extra) * outer
                new[0] = new[0] + (fi - roll_rows(fo, 1))
                new[1] = new[1] + (fo - fi)
                if not which:
                    s0, s1 = trim(sc[0], sw), trim(sc[1], sw)
                    pi = (s1 - s0) * trim(inner, b)
                    po = (roll_rows(s0, -1) - s1) * trim(outer, b)
                    gradient[0] = gradient[0] + (pi + roll_rows(po, 1))
                    gradient[1] = gradient[1] + (pi + po)
            for half in range(2):
                s = trim(sc[half], sw - b)
                v = trim(vc[half], 1)
                new_c[half] = masked(
                    v * ((1.0 + step_dt) - (3.0 * step_dt) * s * s) + new_c[half], b)
                if b:
                    s = trim(sh[half], sw - b)
                    v = trim(vh[half], 1)
                    moved = v * ((1.0 + step_dt) - (3.0 * step_dt) * s * s) + new_h[half]
                    new_h[half] = jnp.where(lane_ok, masked(moved, b - 1), 0.0)
            vc, vh = new_c, new_h
        adjoint = vc

    for half in range(2):
        for x in range(rows):
            where = pl.ds(half * rows + x, 8, stride=2 * rows)
            adjoint_out[where, :] = adjoint[half][x]
            gradient_out[where, :] = gradient[half][x] * (-0.5 * step_dt)

    for g in range(len(fields_of)):
        for m in range(8):
            @pl.when(exists[m])
            def _(g=g, m=m):
                copy(g, m).wait_send()


def per_device(counts, factors, coeffs, diffusivity, terminal):
    thick, rows, lanes = terminal.shape
    steps = coeffs.shape[0]
    width = wide
    rounds = steps // width
    groups = 2 * rounds
    sent = width * (rounds + 1) + sum(width_of(t, width) for t in range(steps))
    flat = (thick * rows, lanes)
    vmem = pl.BlockSpec(memory_space=pltpu.VMEM)
    adjoint, gradient = pl.pallas_call(
        functools.partial(kernel, width, counts),
        out_shape=[jax.ShapeDtypeStruct(flat, jnp.float32)] * 2,
        in_specs=[vmem, pl.BlockSpec(memory_space=pltpu.SMEM), vmem, vmem],
        out_specs=[vmem, vmem],
        scratch_shapes=[
            pltpu.VMEM((steps, *flat), jnp.float32),
            pltpu.VMEM((2, sent, 2, 8, lanes), jnp.float32),
            pltpu.VMEM((2, sent, 2, 8, lanes), jnp.float32),
            pltpu.VMEM((groups, 2, 8, lanes), jnp.float32),
            pltpu.VMEM((6, groups, 2, 8, lanes), jnp.float32),
            pltpu.SemaphoreType.DMA((groups, 8)),
            pltpu.SemaphoreType.DMA((groups, 8)),
        ],
        compiler_params=pltpu.CompilerParams(
            collective_id=0, has_side_effects=True, vmem_limit_bytes=32 * 1024 * 1024
        ),
    )(factors, coeffs, diffusivity.reshape(flat), terminal.reshape(flat))
    return adjoint.reshape(terminal.shape), gradient.reshape(terminal.shape)


def solution(mesh):
    block = P(None, ("groups", "gx"), ("gy", "col"))
    counts = (mesh.shape["gx"], mesh.shape["gy"], mesh.shape["col"])
    return jax.shard_map(
        functools.partial(per_device, counts),
        mesh=mesh,
        in_specs=(
            P(None, None, ("groups", "gx"), ("gy", "col")),
            P("groups", None),
            block,
            block,
        ),
        out_specs=(block, block),
        check_vma=False,
    )
```

```python
import functools

import jax
import jax.numpy as jnp
from jax import lax
from jax.experimental import pallas as pl
from jax.experimental.pallas import tpu as pltpu
from jax.sharding import PartitionSpec as P

step_dt = 0.05
wide = 6

ways = ((-1, 0), (1, 0), (0, 1), (0, -1), (-1, 1), (1, -1), (-1, -1), (1, 1))
opposite = (1, 0, 3, 2, 5, 4, 7, 6)


def roll_lanes(x, shift):
    shift = shift % x.shape[-1]
    return x if shift == 0 else pltpu.roll(x, shift, x.ndim - 1)


def roll_rows(x, shift):
    return pltpu.roll(x, shift % x.shape[-2], x.ndim - 2)


def width_of(step, width):
    return max(1, width - 1 - step % width)


def stride_of(width):
    half = 1
    while half < width:
        half *= 2
    return 2 * half


def state_groups(steps, width):
    groups = []
    for step in range(steps):
        key = (step // width, max(4, stride_of(width_of(step, width))))
        if groups and groups[-1][0] == key:
            groups[-1][1].append(step)
        else:
            groups.append((key, [step]))
    return [names for _, names in groups]


def kernel(
    width, counts, factors_at, coeffs_at, kappa_at, terminal_at, adjoint_out, gradient_out,
    factors, coeffs, kappa_in, terminal, load_sem, natural, row_send, row_recv, pack_send, pack_recv, send_sem, recv_sem,
):
    gx_count, gy_count, col_count = counts
    steps = coeffs.shape[0]
    ranks = factors.shape[0]
    rows = natural.shape[1] // 16
    rounds = steps // width
    group = lax.axis_index("groups")
    gx = lax.axis_index("gx")
    y = lax.axis_index("gy") * col_count + lax.axis_index("col")
    y_count = gy_count * col_count

    def inside(way):
        ok = None
        for at, move, count in ((gx, way[0], gx_count), (y, way[1], y_count)):
            if move == 0:
                continue
            here = at > 0 if move < 0 else at < count - 1
            ok = here if ok is None else jnp.logical_and(ok, here)
        return ok

    def device(way):
        far = y + way[1]
        return (group, gx + way[0], far // col_count, far % col_count)

    exists = [inside(way) for way in ways]

    loads = [
        pltpu.make_async_copy(source, target, load_sem.at[i])
        for i, (source, target) in enumerate(
            ((terminal_at, terminal), (kappa_at, kappa_in), (coeffs_at, coeffs),
             (factors_at, factors)))
    ]
    for copy_in in loads:
        copy_in.start()

    barrier = pltpu.get_barrier_semaphore()
    total = jnp.int32(0)
    for m, way in enumerate(ways):
        @pl.when(exists[m])
        def _(way=way):
            pl.semaphore_signal(
                barrier, inc=1, device_id=device(way), device_id_type=pl.DeviceIdType.MESH
            )
        total = total + exists[m].astype(jnp.int32)

    for m in range(8):
        @pl.when(jnp.logical_not(exists[m]))
        def _(m=m):
            if m < 2:
                row_recv[m] = jnp.zeros(row_recv.shape[1:], jnp.float32)
            else:
                pack_recv[m - 2] = jnp.zeros(pack_recv.shape[1:], jnp.float32)

    spans = {}
    at = 0
    group_rows = []
    by_step = state_groups(steps, width)
    fields_of = [["kappa", "adjoint0"], *by_step]
    for r in range(1, rounds):
        fields_of.append(["adjoint%d" % r])
    group_of = {}
    home = {}
    tiles = 0
    group_tiles = []
    for g, names in enumerate(fields_of):
        start = at
        slot = 0
        for name in names:
            w = width_of(name, width) if isinstance(name, int) else width
            if name == names[0]:
                room = 128 // stride_of(w)
            spans[name] = (at, w)
            home[name] = (tiles + slot // room, slot % room)
            group_of[name] = g
            at += w
            slot += rows
        group_rows.append((start, at - start))
        count = -(-slot // room)
        group_tiles.append((tiles, count))
        tiles += count

    lane = lax.broadcasted_iota(jnp.int32, (8, 128), 1)

    def copy(g, m):
        back = opposite[m]
        if m < 2:
            start, count = group_rows[g]
            source = row_send.at[m, pl.ds(start, count)]
            target = row_recv.at[back, pl.ds(start, count)]
        else:
            start, count = group_tiles[g]
            source = pack_send.at[pl.ds(start, count)]
            target = pack_recv.at[back - 2, pl.ds(start, count)]
        return pltpu.make_async_remote_copy(
            src_ref=source, dst_ref=target,
            send_sem=send_sem.at[g, m], recv_sem=recv_sem.at[g, back],
            device_id=device(ways[m]), device_id_type=pl.DeviceIdType.MESH,
        )

    def pack(g, values):
        names = fields_of[g]
        stride = stride_of(spans[names[0]][1])
        slot_at = ((lane + stride // 2) % 128) // stride
        for half in range(2):
            packed = {}
            for name, value in zip(names, values):
                first, w = spans[name]
                row_send[0, first : first + w, half] = value[half][:w]
                row_send[1, first : first + w, half] = value[half][rows - w :]
                for x in range(rows):
                    tile, slot = home[name][0], home[name][1] + x
                    moved = roll_lanes(value[half][x], slot * stride)
                    packed[tile] = (
                        jnp.where(slot_at == slot, moved, packed[tile])
                        if tile in packed else moved)
            for tile, value in packed.items():
                pack_send[tile, half] = value

    def used(g):
        corners = any(spans[name][1] > 1 for name in fields_of[g])
        return range(8) if corners else range(4)

    def send(g):
        for m in used(g):
            @pl.when(exists[m])
            def _(m=m):
                copy(g, m).start()

    def arrive(g):
        for m in used(g):
            @pl.when(exists[m])
            def _(m=m):
                back = opposite[m]
                if m < 2:
                    start, count = group_rows[g]
                    source = row_send.at[back, pl.ds(start, count)]
                    target = row_recv.at[m, pl.ds(start, count)]
                else:
                    start, count = group_tiles[g]
                    source = pack_send.at[pl.ds(start, count)]
                    target = pack_recv.at[m - 2, pl.ds(start, count)]
                pltpu.make_async_remote_copy(
                    src_ref=source, dst_ref=target,
                    send_sem=send_sem.at[g, back], recv_sem=recv_sem.at[g, m],
                    device_id=device(ways[m]), device_id_type=pl.DeviceIdType.MESH,
                ).wait_recv()

    def padded(name, value):
        g, (tile_at, base) = group_of[name], home[name]
        first, w = spans[name]
        stride = stride_of(spans[fields_of[g][0]][1])
        from_right = lane % stride < stride // 2
        center, halo = [], []
        for half in range(2):
            center.append(jnp.concatenate(
                [row_recv[0, first : first + w, half], value[half],
                 row_recv[1, first : first + w, half]], axis=0))
            own = jnp.where(from_right, pack_recv[0, tile_at, half], pack_recv[1, tile_at, half])
            parts = [(own, range(rows))]
            if w > 1:
                up = jnp.where(from_right, pack_recv[2, tile_at, half], pack_recv[4, tile_at, half])
                down = jnp.where(from_right, pack_recv[5, tile_at, half], pack_recv[3, tile_at, half])
                parts = [(up, range(rows - w + 1, rows)), *parts, (down, range(w - 1))]
            halo.append(jnp.stack(
                [roll_lanes(tile, -(base + x) * stride) for tile, at in parts for x in at]))
        return center, halo

    def load(ref):
        return [
            jnp.stack([ref[pl.ds(half * rows + x, 8, stride=2 * rows), :] for x in range(rows)])
            for half in range(2)
        ]

    def trim(x, extra):
        return x[extra : x.shape[0] - extra] if extra else x

    loads[0].wait()
    adjoint = load(terminal)
    loads[1].wait()
    kappa = [x * (0.5 * step_dt) for x in load(kappa_in)]
    pack(0, [kappa, adjoint])
    pl.semaphore_wait(barrier, total)
    send(0)

    loads[2].wait()
    loads[3].wait()
    states = []
    factor = [factors[k].astype(jnp.float32) for k in range(ranks)]
    for at_group, names in enumerate(by_step):
        for index in names:
            t = steps - 1 - index
            total_state = coeffs[t, 0] * factor[0]
            for k in range(1, ranks):
                total_state = total_state + coeffs[t, k] * factor[k]
            natural[index] = total_state.reshape(natural.shape[1:])
            states.append(load(natural.at[index]))
        pack(1 + at_group, [states[index] for index in names])
        send(1 + at_group)

    last = lane == 127
    start_lane = lane == 0
    near = lane < 64
    lane_ok = jnp.logical_or(
        jnp.logical_and(near, exists[2]), jnp.logical_and(jnp.logical_not(near), exists[3]))

    def ahead(center, halo):
        c, h = roll_lanes(center, -1), roll_lanes(halo, -1)
        return jnp.where(last, h, c), jnp.where(last, c, h)

    def behind(center, halo):
        c, h = roll_lanes(center, 1), roll_lanes(halo, 1)
        return jnp.where(start_lane, h, c), jnp.where(start_lane, c, h)

    def masked(x, b):
        if b == 0:
            return x
        return jnp.concatenate(
            [jnp.where(exists[0], x[:b], 0.0), x[b : b + rows],
             jnp.where(exists[1], x[b + rows :], 0.0)], axis=0)

    arrive(0)
    kc, kh = padded("kappa", kappa)
    face_x = [[x[half][1:] + x[half][:-1] for half in range(2)] for x in (kc, kh)]
    face_y = []
    for half in range(2):
        c = trim(kc[half], 1)
        ca, ha = ahead(c, kh[half])
        face_y.append((c + ca, kh[half] + ha))
    face_z = [(x[0] + x[1], x[1] + roll_rows(x[0], -1)) for x in (kc, kh)]

    gradient = [jnp.zeros((rows, 8, 128), jnp.float32) for _ in range(2)]
    for r in range(rounds):
        if r:
            pack(len(by_step) + r, [adjoint])
            send(len(by_step) + r)
            arrive(len(by_step) + r)
        vc, vh = padded("adjoint%d" % r, adjoint)
        for j in range(width):
            index = r * width + j
            if index == fields_of[group_of[index]][0]:
                arrive(group_of[index])
            a = width - j
            b = a - 1
            skip = width - a
            sc, sh = padded(index, states[index])
            sw = spans[index][1]
            new_c, new_h = [None, None], [None, None]
            for half in range(2):
                d = vc[half][1:] - vc[half][:-1]
                flux = trim(face_x[0][half], skip) * d
                new_c[half] = flux[1:] - flux[:-1]
                ds = trim(sc[half], sw - 1)
                product = (ds[1:] - ds[:-1]) * trim(d, b)
                gradient[half] = gradient[half] + (product[1:] + product[:-1])
                if b:
                    d = vh[half][1:] - vh[half][:-1]
                    flux = trim(face_x[1][half], skip) * d
                    new_h[half] = flux[1:] - flux[:-1]
            for half in range(2):
                c, h = trim(vc[half], 1), vh[half]
                ca, ha = ahead(c, h)
                dc, dh = ca - c, ha - h
                fc = trim(face_y[half][0], skip) * dc
                fh = trim(face_y[half][1], skip) * dh
                bc, bh = behind(fc, fh)
                new_c[half] = new_c[half] + (fc - bc)
                if b:
                    new_h[half] = new_h[half] + trim(fh - bh, 1)
                c, h = trim(sc[half], sw), trim(sh[half], sw - 1)
                ca, ha = ahead(c, h)
                pc = (ca - c) * trim(dc, b)
                ph = (ha - h) * trim(dh, b)
                bc, _ = behind(pc, ph)
                gradient[half] = gradient[half] + (pc + bc)
            for which, v, new, extra in ((0, vc, new_c, skip + 1), (1, vh, new_h, skip + 1)):
                if which and not b:
                    continue
                v0, v1 = trim(v[0], 1), trim(v[1], 1)
                inner, outer = v1 - v0, roll_rows(v0, -1) - v1
                fi = trim(face_z[which][0], extra) * inner
                fo = trim(face_z[which][1], extra) * outer
                new[0] = new[0] + (fi - roll_rows(fo, 1))
                new[1] = new[1] + (fo - fi)
                if not which:
                    s0, s1 = trim(sc[0], sw), trim(sc[1], sw)
                    pi = (s1 - s0) * trim(inner, b)
                    po = (roll_rows(s0, -1) - s1) * trim(outer, b)
                    gradient[0] = gradient[0] + (pi + roll_rows(po, 1))
                    gradient[1] = gradient[1] + (pi + po)
            for half in range(2):
                s = trim(sc[half], sw - b)
                v = trim(vc[half], 1)
                new_c[half] = masked(
                    v * ((1.0 + step_dt) - (3.0 * step_dt) * s * s) + new_c[half], b)
                if b:
                    s = trim(sh[half], sw - b)
                    v = trim(vh[half], 1)
                    moved = v * ((1.0 + step_dt) - (3.0 * step_dt) * s * s) + new_h[half]
                    new_h[half] = jnp.where(lane_ok, masked(moved, b - 1), 0.0)
            vc, vh = new_c, new_h
        adjoint = vc

    for half in range(2):
        for x in range(rows):
            where = pl.ds(half * rows + x, 8, stride=2 * rows)
            adjoint_out[where, :] = adjoint[half][x]
            gradient_out[where, :] = gradient[half][x] * (-0.5 * step_dt)

    for g in range(len(fields_of)):
        for m in used(g):
            @pl.when(exists[m])
            def _(g=g, m=m):
                copy(g, m).wait_send()


def per_device(counts, factors, coeffs, diffusivity, terminal):
    thick, rows, lanes = terminal.shape
    steps = coeffs.shape[0]
    width = wide
    rounds = steps // width
    by_step = state_groups(steps, width)
    groups = len(by_step) + rounds
    tiles = 2 * groups
    sent = width * (rounds + 1) + sum(width_of(t, width) for t in range(steps))
    flat = (thick * rows, lanes)
    vmem = pl.BlockSpec(memory_space=pltpu.VMEM)
    adjoint, gradient = pl.pallas_call(
        functools.partial(kernel, width, counts),
        out_shape=[jax.ShapeDtypeStruct(flat, jnp.float32)] * 2,
        in_specs=[pl.BlockSpec(memory_space=pltpu.HBM)] * 4,
        out_specs=[vmem, vmem],
        scratch_shapes=[
            pltpu.VMEM(factors.shape, factors.dtype),
            pltpu.SMEM(coeffs.shape, jnp.float32),
            pltpu.VMEM(flat, jnp.float32),
            pltpu.VMEM(flat, jnp.float32),
            pltpu.SemaphoreType.DMA((4,)),
            pltpu.VMEM((steps, *flat), jnp.float32),
            pltpu.VMEM((2, sent, 2, 8, lanes), jnp.float32),
            pltpu.VMEM((2, sent, 2, 8, lanes), jnp.float32),
            pltpu.VMEM((tiles, 2, 8, lanes), jnp.float32),
            pltpu.VMEM((6, tiles, 2, 8, lanes), jnp.float32),
            pltpu.SemaphoreType.DMA((groups, 8)),
            pltpu.SemaphoreType.DMA((groups, 8)),
        ],
        compiler_params=pltpu.CompilerParams(
            collective_id=0, has_side_effects=True, vmem_limit_bytes=60 * 1024 * 1024
        ),
    )(factors, coeffs, diffusivity.reshape(flat), terminal.reshape(flat))
    return adjoint.reshape(terminal.shape), gradient.reshape(terminal.shape)


def solution(mesh):
    block = P(None, ("groups", "gx"), ("gy", "col"))
    counts = (mesh.shape["gx"], mesh.shape["gy"], mesh.shape["col"])
    return jax.shard_map(
        functools.partial(per_device, counts),
        mesh=mesh,
        in_specs=(
            P(None, None, ("groups", "gx"), ("gy", "col")),
            P("groups", None),
            block,
            block,
        ),
        out_specs=(block, block),
        check_vma=False,
    )
```

```python
import functools

import jax
import jax.numpy as jnp
from jax import lax
from jax.experimental import pallas as pl
from jax.experimental.pallas import tpu as pltpu
from jax.sharding import PartitionSpec as P

step_dt = 0.05
wide = 6

ways = ((-1, 0), (1, 0), (0, 1), (0, -1), (-1, 1), (1, -1), (-1, -1), (1, 1))
opposite = (1, 0, 3, 2, 5, 4, 7, 6)


def roll_lanes(x, shift):
    shift = shift % x.shape[-1]
    return x if shift == 0 else pltpu.roll(x, shift, x.ndim - 1)


def roll_rows(x, shift):
    return pltpu.roll(x, shift % x.shape[-2], x.ndim - 2)


def width_of(step, width):
    return max(1, width - 1 - step % width)


def stride_of(width):
    half = 1
    while half < width:
        half *= 2
    return 2 * half


def near_rows(name):
    return 2 if isinstance(name, str) and name.startswith("adjoint") else 1


def state_groups(steps, width):
    groups = []
    for step in range(steps):
        key = (step // width, max(4, stride_of(width_of(step, width))))
        if groups and groups[-1][0] == key:
            groups[-1][1].append(step)
        else:
            groups.append((key, [step]))
    return [names for _, names in groups]


def kernel(
    width, counts, factors_at, coeffs_at, kappa_at, terminal_at, adjoint_out, gradient_out,
    factors, coeffs, kappa_in, terminal, load_sem, natural, row_send, row_recv, low_send, low_recv, pack_send, pack_recv, corner_send,
    corner_recv, send_sem, recv_sem,
):
    gx_count, gy_count, col_count = counts
    steps = coeffs.shape[0]
    ranks = factors.shape[0]
    rows = natural.shape[1] // 16
    rounds = steps // width
    group = lax.axis_index("groups")
    gx = lax.axis_index("gx")
    y = lax.axis_index("gy") * col_count + lax.axis_index("col")
    y_count = gy_count * col_count

    def inside(way):
        ok = None
        for at, move, count in ((gx, way[0], gx_count), (y, way[1], y_count)):
            if move == 0:
                continue
            here = at > 0 if move < 0 else at < count - 1
            ok = here if ok is None else jnp.logical_and(ok, here)
        return ok

    def device(way):
        far = y + way[1]
        return (group, gx + way[0], far // col_count, far % col_count)

    exists = [inside(way) for way in ways]

    loads = [
        pltpu.make_async_copy(source, target, load_sem.at[i])
        for i, (source, target) in enumerate(
            ((terminal_at, terminal), (kappa_at, kappa_in), (coeffs_at, coeffs),
             (factors_at, factors)))
    ]
    for copy_in in loads:
        copy_in.start()

    barrier = pltpu.get_barrier_semaphore()
    total = jnp.int32(0)
    for m, way in enumerate(ways):
        @pl.when(exists[m])
        def _(way=way):
            pl.semaphore_signal(
                barrier, inc=1, device_id=device(way), device_id_type=pl.DeviceIdType.MESH
            )
        total = total + exists[m].astype(jnp.int32)

    for m in range(8):
        @pl.when(jnp.logical_not(exists[m]))
        def _(m=m):
            if m < 2:
                row_recv[m] = jnp.zeros(row_recv.shape[1:], jnp.float32)
                low_recv[m] = jnp.zeros(low_recv.shape[1:], jnp.bfloat16)
            elif m < 4:
                pack_recv[m - 2] = jnp.zeros(pack_recv.shape[1:], jnp.float32)
            else:
                corner_recv[m - 4] = jnp.zeros(corner_recv.shape[1:], jnp.bfloat16)

    spans = {}
    at = low_at = 0
    group_rows = []
    low_rows = []
    lows = {}
    by_step = state_groups(steps, width)
    fields_of = [["kappa", "adjoint0"], *by_step]
    for r in range(1, rounds):
        fields_of.append(["adjoint%d" % r])
    group_of = {}
    home = {}
    tiles = 0
    group_tiles = []
    for g, names in enumerate(fields_of):
        row_start, low_start = at, low_at
        slot = 0
        for name in names:
            w = width_of(name, width) if isinstance(name, int) else width
            if name == names[0]:
                room = 128 // stride_of(w)
            spans[name] = (at, w)
            home[name] = (tiles + slot // room, slot % room)
            group_of[name] = g
            near = min(w, near_rows(name))
            lows[name] = (low_at, near)
            at += near
            low_at += w - near
            slot += rows
        group_rows.append((row_start, at - row_start))
        low_rows.append((low_start, low_at - low_start))
        count = -(-slot // room)
        group_tiles.append((tiles, count))
        tiles += count

    lane = lax.broadcasted_iota(jnp.int32, (8, 128), 1)

    def refs(g, m, to):
        if m < 2:
            span = pl.ds(*group_rows[g])
            return row_send.at[m, span], row_recv.at[to, span]
        if m >= 8:
            span = pl.ds(*low_rows[g])
            return low_send.at[m - 8, span], low_recv.at[to - 8, span]
        span = pl.ds(*group_tiles[g])
        if m < 4:
            return pack_send.at[span], pack_recv.at[to - 2, span]
        return corner_send.at[span], corner_recv.at[to - 4, span]

    def turned(m):
        return 17 - m if m >= 8 else opposite[m]

    def copy(g, m, arriving=False):
        leaves, lands = (turned(m), m) if arriving else (m, turned(m))
        source, target = refs(g, leaves, lands)
        return pltpu.make_async_remote_copy(
            src_ref=source, dst_ref=target,
            send_sem=send_sem.at[g, leaves], recv_sem=recv_sem.at[g, lands],
            device_id=device(ways[m % 8]), device_id_type=pl.DeviceIdType.MESH,
        )

    def pack(g, values):
        names = fields_of[g]
        stride = stride_of(spans[names[0]][1])
        slot_at = ((lane + stride // 2) % 128) // stride
        packed = [{}, {}]
        for name, value in zip(names, values):
            (first, w), (low_first, near) = spans[name], lows[name]
            for half in range(2):
                row_send[0, first : first + near, half] = value[half][:near]
                row_send[1, first : first + near, half] = value[half][rows - near :]
                for x in range(rows):
                    tile, slot = home[name][0], home[name][1] + x
                    moved = roll_lanes(value[half][x], slot * stride)
                    held = packed[half]
                    held[tile] = (
                        jnp.where(slot_at == slot, moved, held[tile]) if tile in held else moved)
            if w > near:
                both = jnp.concatenate(value, axis=1).astype(jnp.bfloat16)
                low_send[0, low_first : low_first + w - near] = both[near:w]
                low_send[1, low_first : low_first + w - near] = both[rows - w : rows - near]
        for tile in packed[0]:
            pack_send[tile, 0] = packed[0][tile]
            pack_send[tile, 1] = packed[1][tile]
            both = jnp.concatenate([packed[0][tile], packed[1][tile]], axis=0)
            corner_send[tile] = both.astype(jnp.bfloat16)

    def used(g):
        corners = any(spans[name][1] > 1 for name in fields_of[g])
        messages = list(range(2))
        if low_rows[g][1]:
            messages += [8, 9]
        return messages + list(range(2, 8 if corners else 4))

    def send(g):
        for m in used(g):
            @pl.when(exists[m % 8])
            def _(m=m):
                copy(g, m).start()

    def arrive(g):
        for m in used(g):
            @pl.when(exists[m % 8])
            def _(m=m):
                copy(g, m, arriving=True).wait_recv()

    def padded(name, value):
        g, (tile_at, base) = group_of[name], home[name]
        first, w = spans[name]
        stride = stride_of(spans[fields_of[g][0]][1])
        from_right = lane % stride < stride // 2
        low_first, near = lows[name]
        center, halo = [], []
        outer = [[], []]
        if w > near:
            outer = [
                [low_recv[side, low_first : low_first + w - near].astype(jnp.float32)]
                for side in range(2)
            ]

        def corner(way, half):
            return corner_recv[way - 4, tile_at].astype(jnp.float32)[8 * half : 8 * half + 8]

        for half in range(2):
            part = slice(8 * half, 8 * half + 8)
            center.append(jnp.concatenate(
                [*(x[:, part] for x in outer[0]), row_recv[0, first : first + near, half],
                 value[half], row_recv[1, first : first + near, half],
                 *(x[:, part] for x in outer[1])], axis=0))
            own = jnp.where(from_right, pack_recv[0, tile_at, half], pack_recv[1, tile_at, half])
            parts = [(own, range(rows))]
            if w > 1:
                up = jnp.where(from_right, corner(4, half), corner(6, half))
                down = jnp.where(from_right, corner(7, half), corner(5, half))
                parts = [(up, range(rows - w + 1, rows)), *parts, (down, range(w - 1))]
            halo.append(jnp.stack(
                [roll_lanes(tile, -(base + x) * stride) for tile, at in parts for x in at]))
        return center, halo

    def load(ref):
        return [
            jnp.stack([ref[pl.ds(half * rows + x, 8, stride=2 * rows), :] for x in range(rows)])
            for half in range(2)
        ]

    def trim(x, extra):
        return x[extra : x.shape[0] - extra] if extra else x

    loads[0].wait()
    adjoint = load(terminal)
    loads[1].wait()
    kappa = [x * (0.5 * step_dt) for x in load(kappa_in)]
    pack(0, [kappa, adjoint])
    pl.semaphore_wait(barrier, total)
    send(0)

    loads[2].wait()
    loads[3].wait()
    states = []
    factor = [factors[k].astype(jnp.float32) for k in range(ranks)]
    for at_group, names in enumerate(by_step):
        for index in names:
            t = steps - 1 - index
            total_state = coeffs[t, 0] * factor[0]
            for k in range(1, ranks):
                total_state = total_state + coeffs[t, k] * factor[k]
            natural[index] = total_state.reshape(natural.shape[1:])
            states.append(load(natural.at[index]))
        pack(1 + at_group, [states[index] for index in names])
        send(1 + at_group)

    last = lane == 127
    start_lane = lane == 0
    near = lane < 64
    lane_ok = jnp.logical_or(
        jnp.logical_and(near, exists[2]), jnp.logical_and(jnp.logical_not(near), exists[3]))

    def ahead(center, halo):
        c, h = roll_lanes(center, -1), roll_lanes(halo, -1)
        return jnp.where(last, h, c), jnp.where(last, c, h)

    def behind(center, halo):
        c, h = roll_lanes(center, 1), roll_lanes(halo, 1)
        return jnp.where(start_lane, h, c), jnp.where(start_lane, c, h)

    def masked(x, b):
        if b == 0:
            return x
        return jnp.concatenate(
            [jnp.where(exists[0], x[:b], 0.0), x[b : b + rows],
             jnp.where(exists[1], x[b + rows :], 0.0)], axis=0)

    arrive(0)
    kc, kh = padded("kappa", kappa)
    face_x = [[x[half][1:] + x[half][:-1] for half in range(2)] for x in (kc, kh)]
    face_y = []
    for half in range(2):
        c = trim(kc[half], 1)
        ca, ha = ahead(c, kh[half])
        face_y.append((c + ca, kh[half] + ha))
    face_z = [(x[0] + x[1], x[1] + roll_rows(x[0], -1)) for x in (kc, kh)]

    gradient = [jnp.zeros((rows, 8, 128), jnp.float32) for _ in range(2)]
    for r in range(rounds):
        if r:
            pack(len(by_step) + r, [adjoint])
            send(len(by_step) + r)
            arrive(len(by_step) + r)
        vc, vh = padded("adjoint%d" % r, adjoint)
        for j in range(width):
            index = r * width + j
            if index == fields_of[group_of[index]][0]:
                arrive(group_of[index])
            a = width - j
            b = a - 1
            skip = width - a
            sc, sh = padded(index, states[index])
            sw = spans[index][1]
            new_c, new_h = [None, None], [None, None]
            for half in range(2):
                d = vc[half][1:] - vc[half][:-1]
                flux = trim(face_x[0][half], skip) * d
                new_c[half] = flux[1:] - flux[:-1]
                ds = trim(sc[half], sw - 1)
                product = (ds[1:] - ds[:-1]) * trim(d, b)
                gradient[half] = gradient[half] + (product[1:] + product[:-1])
                if b:
                    d = vh[half][1:] - vh[half][:-1]
                    flux = trim(face_x[1][half], skip) * d
                    new_h[half] = flux[1:] - flux[:-1]
            for half in range(2):
                c, h = trim(vc[half], 1), vh[half]
                ca, ha = ahead(c, h)
                dc, dh = ca - c, ha - h
                fc = trim(face_y[half][0], skip) * dc
                fh = trim(face_y[half][1], skip) * dh
                bc, bh = behind(fc, fh)
                new_c[half] = new_c[half] + (fc - bc)
                if b:
                    new_h[half] = new_h[half] + trim(fh - bh, 1)
                c, h = trim(sc[half], sw), trim(sh[half], sw - 1)
                ca, ha = ahead(c, h)
                pc = (ca - c) * trim(dc, b)
                ph = (ha - h) * trim(dh, b)
                bc, _ = behind(pc, ph)
                gradient[half] = gradient[half] + (pc + bc)
            for which, v, new, extra in ((0, vc, new_c, skip + 1), (1, vh, new_h, skip + 1)):
                if which and not b:
                    continue
                v0, v1 = trim(v[0], 1), trim(v[1], 1)
                inner, outer = v1 - v0, roll_rows(v0, -1) - v1
                fi = trim(face_z[which][0], extra) * inner
                fo = trim(face_z[which][1], extra) * outer
                new[0] = new[0] + (fi - roll_rows(fo, 1))
                new[1] = new[1] + (fo - fi)
                if not which:
                    s0, s1 = trim(sc[0], sw), trim(sc[1], sw)
                    pi = (s1 - s0) * trim(inner, b)
                    po = (roll_rows(s0, -1) - s1) * trim(outer, b)
                    gradient[0] = gradient[0] + (pi + roll_rows(po, 1))
                    gradient[1] = gradient[1] + (pi + po)
            for half in range(2):
                s = trim(sc[half], sw - b)
                v = trim(vc[half], 1)
                new_c[half] = masked(
                    v * ((1.0 + step_dt) - (3.0 * step_dt) * s * s) + new_c[half], b)
                if b:
                    s = trim(sh[half], sw - b)
                    v = trim(vh[half], 1)
                    moved = v * ((1.0 + step_dt) - (3.0 * step_dt) * s * s) + new_h[half]
                    new_h[half] = jnp.where(lane_ok, masked(moved, b - 1), 0.0)
            vc, vh = new_c, new_h
        adjoint = vc

    for half in range(2):
        for x in range(rows):
            where = pl.ds(half * rows + x, 8, stride=2 * rows)
            adjoint_out[where, :] = adjoint[half][x]
            gradient_out[where, :] = gradient[half][x] * (-0.5 * step_dt)

    for g in range(len(fields_of)):
        for m in used(g):
            @pl.when(exists[m % 8])
            def _(g=g, m=m):
                copy(g, m).wait_send()


def per_device(counts, factors, coeffs, diffusivity, terminal):
    thick, rows, lanes = terminal.shape
    steps = coeffs.shape[0]
    width = wide
    rounds = steps // width
    by_step = state_groups(steps, width)
    groups = len(by_step) + rounds
    tiles = 2 * groups
    fields = ["kappa", *("adjoint%d" % r for r in range(rounds)), *range(steps)]
    widths = [width if isinstance(name, str) else width_of(name, width) for name in fields]
    near = sum(min(w, near_rows(name)) for w, name in zip(widths, fields))
    far = max(1, sum(widths) - near)
    flat = (thick * rows, lanes)
    vmem = pl.BlockSpec(memory_space=pltpu.VMEM)
    adjoint, gradient = pl.pallas_call(
        functools.partial(kernel, width, counts),
        out_shape=[jax.ShapeDtypeStruct(flat, jnp.float32)] * 2,
        in_specs=[pl.BlockSpec(memory_space=pltpu.HBM)] * 4,
        out_specs=[vmem, vmem],
        scratch_shapes=[
            pltpu.VMEM(factors.shape, factors.dtype),
            pltpu.SMEM(coeffs.shape, jnp.float32),
            pltpu.VMEM(flat, jnp.float32),
            pltpu.VMEM(flat, jnp.float32),
            pltpu.SemaphoreType.DMA((4,)),
            pltpu.VMEM((steps, *flat), jnp.float32),
            pltpu.VMEM((2, near, 2, 8, lanes), jnp.float32),
            pltpu.VMEM((2, near, 2, 8, lanes), jnp.float32),
            pltpu.VMEM((2, far, 16, lanes), jnp.bfloat16),
            pltpu.VMEM((2, far, 16, lanes), jnp.bfloat16),
            pltpu.VMEM((tiles, 2, 8, lanes), jnp.float32),
            pltpu.VMEM((2, tiles, 2, 8, lanes), jnp.float32),
            pltpu.VMEM((tiles, 16, lanes), jnp.bfloat16),
            pltpu.VMEM((4, tiles, 16, lanes), jnp.bfloat16),
            pltpu.SemaphoreType.DMA((groups, 10)),
            pltpu.SemaphoreType.DMA((groups, 10)),
        ],
        compiler_params=pltpu.CompilerParams(
            collective_id=0, has_side_effects=True, vmem_limit_bytes=60 * 1024 * 1024
        ),
    )(factors, coeffs, diffusivity.reshape(flat), terminal.reshape(flat))
    return adjoint.reshape(terminal.shape), gradient.reshape(terminal.shape)


def solution(mesh):
    block = P(None, ("groups", "gx"), ("gy", "col"))
    counts = (mesh.shape["gx"], mesh.shape["gy"], mesh.shape["col"])
    return jax.shard_map(
        functools.partial(per_device, counts),
        mesh=mesh,
        in_specs=(
            P(None, None, ("groups", "gx"), ("gy", "col")),
            P("groups", None),
            block,
            block,
        ),
        out_specs=(block, block),
        check_vma=False,
    )
```

```python
import functools

import jax
import jax.numpy as jnp
from jax import lax
from jax.experimental import pallas as pl
from jax.experimental.pallas import tpu as pltpu
from jax.sharding import PartitionSpec as P

step_dt = 0.05
wide = 6

ways = ((-1, 0), (1, 0), (0, 1), (0, -1), (-1, 1), (1, -1), (-1, -1), (1, 1))
opposite = (1, 0, 3, 2, 5, 4, 7, 6)


def roll_lanes(x, shift):
    shift = shift % x.shape[-1]
    return x if shift == 0 else pltpu.roll(x, shift, x.ndim - 1)


def roll_rows(x, shift):
    return pltpu.roll(x, shift % x.shape[-2], x.ndim - 2)


def width_of(step, width):
    return max(1, width - 1 - step % width)


def stride_of(width):
    half = 1
    while half < width:
        half *= 2
    return 2 * half


def near_rows(name):
    return 2 if isinstance(name, str) and name.startswith("adjoint") else 1


def state_groups(steps, width):
    groups = []
    for step in range(steps):
        key = (step // width, max(4, stride_of(width_of(step, width))))
        if groups and groups[-1][0] == key:
            groups[-1][1].append(step)
        else:
            groups.append((key, [step]))
    return [names for _, names in groups]


def kernel(
    width, counts, factors_at, coeffs_at, kappa_at, terminal_at, adjoint_out, gradient_out,
    factors, coeffs, kappa_in, terminal, load_sem, natural, row_send, row_recv, low_send, low_recv, pack_send, pack_recv, corner_send,
    corner_recv, send_sem, recv_sem,
):
    gx_count, gy_count, col_count = counts
    steps = coeffs.shape[0]
    ranks = factors.shape[0]
    rows = natural.shape[1] // 16
    rounds = steps // width
    group = lax.axis_index("groups")
    gx = lax.axis_index("gx")
    y = lax.axis_index("gy") * col_count + lax.axis_index("col")
    y_count = gy_count * col_count

    def inside(way):
        ok = None
        for at, move, count in ((gx, way[0], gx_count), (y, way[1], y_count)):
            if move == 0:
                continue
            here = at > 0 if move < 0 else at < count - 1
            ok = here if ok is None else jnp.logical_and(ok, here)
        return ok

    def device(way):
        far = y + way[1]
        return (group, gx + way[0], far // col_count, far % col_count)

    exists = [inside(way) for way in ways]

    loads = [
        pltpu.make_async_copy(source, target, load_sem.at[i])
        for i, (source, target) in enumerate(
            ((terminal_at, terminal), (kappa_at, kappa_in), (coeffs_at, coeffs),
             (factors_at, factors)))
    ]
    for copy_in in loads:
        copy_in.start()

    barrier = pltpu.get_barrier_semaphore()
    total = jnp.int32(0)
    for m, way in enumerate(ways):
        @pl.when(exists[m])
        def _(way=way):
            pl.semaphore_signal(
                barrier, inc=1, device_id=device(way), device_id_type=pl.DeviceIdType.MESH
            )
        total = total + exists[m].astype(jnp.int32)

    for m in range(8):
        @pl.when(jnp.logical_not(exists[m]))
        def _(m=m):
            if m < 2:
                row_recv[m] = jnp.zeros(row_recv.shape[1:], jnp.float32)
                low_recv[m] = jnp.zeros(low_recv.shape[1:], jnp.bfloat16)
            elif m < 4:
                pack_recv[m - 2] = jnp.zeros(pack_recv.shape[1:], jnp.float32)
            else:
                corner_recv[m - 4] = jnp.zeros(corner_recv.shape[1:], jnp.bfloat16)

    spans = {}
    at = low_at = 0
    group_rows = []
    low_rows = []
    lows = {}
    by_step = state_groups(steps, width)
    fields_of = [["kappa", "adjoint0"], *by_step]
    for r in range(1, rounds):
        fields_of.append(["adjoint%d" % r])
    group_of = {}
    home = {}
    tiles = 0
    group_tiles = []
    for g, names in enumerate(fields_of):
        row_start, low_start = at, low_at
        slot = 0
        for name in names:
            w = width_of(name, width) if isinstance(name, int) else width
            if name == names[0]:
                room = 128 // stride_of(w)
            spans[name] = (at, w)
            home[name] = (tiles + slot // room, slot % room)
            group_of[name] = g
            near = min(w, near_rows(name))
            lows[name] = (low_at, near)
            at += near
            low_at += w - near
            slot += rows
        group_rows.append((row_start, at - row_start))
        low_rows.append((low_start, low_at - low_start))
        count = -(-slot // room)
        group_tiles.append((tiles, count))
        tiles += count

    lane = lax.broadcasted_iota(jnp.int32, (8, 128), 1)

    def refs(g, m, to):
        if m < 2:
            span = pl.ds(*group_rows[g])
            return row_send.at[m, span], row_recv.at[to, span]
        if m >= 8:
            span = pl.ds(*low_rows[g])
            return low_send.at[m - 8, span], low_recv.at[to - 8, span]
        span = pl.ds(*group_tiles[g])
        if m < 4:
            return pack_send.at[span], pack_recv.at[to - 2, span]
        return corner_send.at[span], corner_recv.at[to - 4, span]

    def turned(m):
        return 17 - m if m >= 8 else opposite[m]

    def copy(g, m, arriving=False):
        leaves, lands = (turned(m), m) if arriving else (m, turned(m))
        source, target = refs(g, leaves, lands)
        return pltpu.make_async_remote_copy(
            src_ref=source, dst_ref=target,
            send_sem=send_sem.at[g, leaves], recv_sem=recv_sem.at[g, lands],
            device_id=device(ways[m % 8]), device_id_type=pl.DeviceIdType.MESH,
        )

    def pack(g, values):
        names = fields_of[g]
        stride = stride_of(spans[names[0]][1])
        slot_at = ((lane + stride // 2) % 128) // stride
        packed = [{}, {}]
        for name, value in zip(names, values):
            (first, w), (low_first, near) = spans[name], lows[name]
            for half in range(2):
                row_send[0, first : first + near, half] = value[half][:near]
                row_send[1, first : first + near, half] = value[half][rows - near :]
                for x in range(rows):
                    tile, slot = home[name][0], home[name][1] + x
                    moved = roll_lanes(value[half][x], slot * stride)
                    held = packed[half]
                    held[tile] = (
                        jnp.where(slot_at == slot, moved, held[tile]) if tile in held else moved)
            if w > near:
                both = jnp.concatenate(value, axis=1).astype(jnp.bfloat16)
                low_send[0, low_first : low_first + w - near] = both[near:w]
                low_send[1, low_first : low_first + w - near] = both[rows - w : rows - near]
        for tile in packed[0]:
            pack_send[tile, 0] = packed[0][tile]
            pack_send[tile, 1] = packed[1][tile]
            both = jnp.concatenate([packed[0][tile], packed[1][tile]], axis=0)
            corner_send[tile] = both.astype(jnp.bfloat16)

    def used(g):
        corners = any(spans[name][1] > 1 for name in fields_of[g])
        messages = list(range(2))
        if low_rows[g][1]:
            messages += [8, 9]
        return messages + list(range(2, 8 if corners else 4))

    def send(g):
        for m in used(g):
            @pl.when(exists[m % 8])
            def _(m=m):
                copy(g, m).start()

    def arrive(g):
        for m in used(g):
            @pl.when(exists[m % 8])
            def _(m=m):
                copy(g, m, arriving=True).wait_recv()

    def padded(name, value):
        g, (tile_at, base) = group_of[name], home[name]
        first, w = spans[name]
        stride = stride_of(spans[fields_of[g][0]][1])
        from_right = lane % stride < stride // 2
        low_first, near = lows[name]
        center, halo = [], []
        outer = [[], []]
        if w > near:
            outer = [
                [low_recv[side, low_first : low_first + w - near].astype(jnp.float32)]
                for side in range(2)
            ]

        def corner(way, half):
            return corner_recv[way - 4, tile_at].astype(jnp.float32)[8 * half : 8 * half + 8]

        for half in range(2):
            part = slice(8 * half, 8 * half + 8)
            center.append(jnp.concatenate(
                [*(x[:, part] for x in outer[0]), row_recv[0, first : first + near, half],
                 value[half], row_recv[1, first : first + near, half],
                 *(x[:, part] for x in outer[1])], axis=0))
            own = jnp.where(from_right, pack_recv[0, tile_at, half], pack_recv[1, tile_at, half])
            parts = [(own, range(rows))]
            if w > 1:
                up = jnp.where(from_right, corner(4, half), corner(6, half))
                down = jnp.where(from_right, corner(7, half), corner(5, half))
                parts = [(up, range(rows - w + 1, rows)), *parts, (down, range(w - 1))]
            halo.append(jnp.stack(
                [roll_lanes(tile, -(base + x) * stride) for tile, at in parts for x in at]))
        return center, halo

    def load(ref):
        return [
            jnp.stack([ref[pl.ds(half * rows + x, 8, stride=2 * rows), :] for x in range(rows)])
            for half in range(2)
        ]

    def trim(x, extra):
        return x[extra : x.shape[0] - extra] if extra else x

    loads[0].wait()
    adjoint = load(terminal)
    loads[1].wait()
    kappa = [x * (0.5 * step_dt) for x in load(kappa_in)]
    pack(0, [kappa, adjoint])
    pl.semaphore_wait(barrier, total)
    send(0)

    loads[2].wait()
    loads[3].wait()
    states = []
    factor = [factors[k].astype(jnp.float32) for k in range(ranks)]
    for at_group, names in enumerate(by_step):
        for index in names:
            t = steps - 1 - index
            total_state = coeffs[t, 0] * factor[0]
            for k in range(1, ranks):
                total_state = total_state + coeffs[t, k] * factor[k]
            natural[index] = total_state.reshape(natural.shape[1:])
            states.append(load(natural.at[index]))
        pack(1 + at_group, [states[index] for index in names])
        send(1 + at_group)

    last = lane == 127
    start_lane = lane == 0
    near = lane < 64
    lane_ok = jnp.logical_or(
        jnp.logical_and(near, exists[2]), jnp.logical_and(jnp.logical_not(near), exists[3]))

    def ahead(center, halo):
        c, h = roll_lanes(center, -1), roll_lanes(halo, -1)
        return jnp.where(last, h, c), jnp.where(last, c, h)

    def behind(center, halo):
        c, h = roll_lanes(center, 1), roll_lanes(halo, 1)
        return jnp.where(start_lane, h, c), jnp.where(start_lane, c, h)

    def masked(x, b):
        if b == 0:
            return x
        return jnp.concatenate(
            [jnp.where(exists[0], x[:b], 0.0), x[b : b + rows],
             jnp.where(exists[1], x[b + rows :], 0.0)], axis=0)

    arrive(0)
    kc, kh = padded("kappa", kappa)
    face_x = [[x[half][1:] + x[half][:-1] for half in range(2)] for x in (kc, kh)]
    face_y = []
    for half in range(2):
        c = trim(kc[half], 1)
        ca, ha = ahead(c, kh[half])
        face_y.append((c + ca, kh[half] + ha))
    face_z = [(x[0] + x[1], x[1] + roll_rows(x[0], -1)) for x in (kc, kh)]

    gradient = [jnp.zeros((rows, 8, 128), jnp.float32) for _ in range(2)]
    for r in range(rounds):
        if r:
            pack(len(by_step) + r, [adjoint])
            send(len(by_step) + r)
            arrive(len(by_step) + r)
        vc, vh = padded("adjoint%d" % r, adjoint)
        for j in range(width):
            index = r * width + j
            if index == fields_of[group_of[index]][0]:
                arrive(group_of[index])
            a = width - j
            b = a - 1
            skip = width - a
            sc, sh = padded(index, states[index])
            sw = spans[index][1]
            new_c, new_h = [None, None], [None, None]
            for half in range(2):
                d = vc[half][1:] - vc[half][:-1]
                flux = trim(face_x[0][half], skip) * d
                new_c[half] = flux[1:] - flux[:-1]
                ds = trim(sc[half], sw - 1)
                product = (ds[1:] - ds[:-1]) * trim(d, b)
                gradient[half] = gradient[half] + (product[1:] + product[:-1])
                if b:
                    d = vh[half][1:] - vh[half][:-1]
                    flux = trim(face_x[1][half], skip) * d
                    new_h[half] = flux[1:] - flux[:-1]
            for half in range(2):
                c, h = trim(vc[half], 1), vh[half]
                ca, ha = ahead(c, h)
                dc, dh = ca - c, ha - h
                fc = trim(face_y[half][0], skip) * dc
                fh = trim(face_y[half][1], skip) * dh
                bc, bh = behind(fc, fh)
                new_c[half] = new_c[half] + (fc - bc)
                if b:
                    new_h[half] = new_h[half] + trim(fh - bh, 1)
                c, h = trim(sc[half], sw), trim(sh[half], sw - 1)
                ca, ha = ahead(c, h)
                pc = (ca - c) * trim(dc, b)
                ph = (ha - h) * trim(dh, b)
                bc, _ = behind(pc, ph)
                gradient[half] = gradient[half] + (pc + bc)
            for which, v, new, extra in ((0, vc, new_c, skip + 1), (1, vh, new_h, skip + 1)):
                if which and not b:
                    continue
                v0, v1 = trim(v[0], 1), trim(v[1], 1)
                inner, outer = v1 - v0, roll_rows(v0, -1) - v1
                fi = trim(face_z[which][0], extra) * inner
                fo = trim(face_z[which][1], extra) * outer
                new[0] = new[0] + (fi - roll_rows(fo, 1))
                new[1] = new[1] + (fo - fi)
                if not which:
                    s0, s1 = trim(sc[0], sw), trim(sc[1], sw)
                    pi = (s1 - s0) * trim(inner, b)
                    po = (roll_rows(s0, -1) - s1) * trim(outer, b)
                    gradient[0] = gradient[0] + (pi + roll_rows(po, 1))
                    gradient[1] = gradient[1] + (pi + po)
            for half in range(2):
                s = trim(sc[half], sw - b)
                v = trim(vc[half], 1)
                new_c[half] = masked(
                    v * ((1.0 + step_dt) - (3.0 * step_dt) * s * s) + new_c[half], b)
                if b:
                    s = trim(sh[half], sw - b)
                    v = trim(vh[half], 1)
                    moved = v * ((1.0 + step_dt) - (3.0 * step_dt) * s * s) + new_h[half]
                    new_h[half] = jnp.where(lane_ok, masked(moved, b - 1), 0.0)
            vc, vh = new_c, new_h
        adjoint = vc

    for half in range(2):
        for x in range(rows):
            where = pl.ds(half * rows + x, 8, stride=2 * rows)
            adjoint_out[where, :] = adjoint[half][x]
            gradient_out[where, :] = gradient[half][x] * (-0.5 * step_dt)

    for g in range(len(fields_of)):
        for m in used(g):
            @pl.when(exists[m % 8])
            def _(g=g, m=m):
                copy(g, m).wait_send()


def store(adjoint, gradient, adjoint_out, gradient_out, sem):
    copies = [
        pltpu.make_async_copy(adjoint, adjoint_out, sem.at[0]),
        pltpu.make_async_copy(gradient, gradient_out, sem.at[1]),
    ]
    for copy in copies:
        copy.start()
    for copy in copies:
        copy.wait()


def per_device(counts, factors, coeffs, diffusivity, terminal):
    thick, rows, lanes = terminal.shape
    steps = coeffs.shape[0]
    width = wide
    rounds = steps // width
    by_step = state_groups(steps, width)
    groups = len(by_step) + rounds
    tiles = 2 * groups
    fields = ["kappa", *("adjoint%d" % r for r in range(rounds)), *range(steps)]
    widths = [width if isinstance(name, str) else width_of(name, width) for name in fields]
    near = sum(min(w, near_rows(name)) for w, name in zip(widths, fields))
    far = max(1, sum(widths) - near)
    flat = (thick * rows, lanes)
    vmem = pl.BlockSpec(memory_space=pltpu.VMEM)
    adjoint, gradient = pl.pallas_call(
        functools.partial(kernel, width, counts),
        out_shape=[jax.ShapeDtypeStruct(flat, jnp.float32)] * 2,
        in_specs=[pl.BlockSpec(memory_space=pltpu.HBM)] * 4,
        out_specs=[vmem, vmem],
        scratch_shapes=[
            pltpu.VMEM(factors.shape, factors.dtype),
            pltpu.SMEM(coeffs.shape, jnp.float32),
            pltpu.VMEM(flat, jnp.float32),
            pltpu.VMEM(flat, jnp.float32),
            pltpu.SemaphoreType.DMA((4,)),
            pltpu.VMEM((steps, *flat), jnp.float32),
            pltpu.VMEM((2, near, 2, 8, lanes), jnp.float32),
            pltpu.VMEM((2, near, 2, 8, lanes), jnp.float32),
            pltpu.VMEM((2, far, 16, lanes), jnp.bfloat16),
            pltpu.VMEM((2, far, 16, lanes), jnp.bfloat16),
            pltpu.VMEM((tiles, 2, 8, lanes), jnp.float32),
            pltpu.VMEM((2, tiles, 2, 8, lanes), jnp.float32),
            pltpu.VMEM((tiles, 16, lanes), jnp.bfloat16),
            pltpu.VMEM((4, tiles, 16, lanes), jnp.bfloat16),
            pltpu.SemaphoreType.DMA((groups, 10)),
            pltpu.SemaphoreType.DMA((groups, 10)),
        ],
        compiler_params=pltpu.CompilerParams(
            collective_id=0, has_side_effects=True, vmem_limit_bytes=60 * 1024 * 1024
        ),
    )(factors, coeffs, diffusivity.reshape(flat), terminal.reshape(flat))
    adjoint, gradient = pl.pallas_call(
        store,
        out_shape=[jax.ShapeDtypeStruct(flat, jnp.float32)] * 2,
        in_specs=[vmem] * 2,
        out_specs=[pl.BlockSpec(memory_space=pltpu.HBM)] * 2,
        scratch_shapes=[pltpu.SemaphoreType.DMA((2,))],
    )(adjoint, gradient)
    return adjoint.reshape(terminal.shape), gradient.reshape(terminal.shape)


def solution(mesh):
    block = P(None, ("groups", "gx"), ("gy", "col"))
    counts = (mesh.shape["gx"], mesh.shape["gy"], mesh.shape["col"])
    return jax.shard_map(
        functools.partial(per_device, counts),
        mesh=mesh,
        in_specs=(
            P(None, None, ("groups", "gx"), ("gy", "col")),
            P("groups", None),
            block,
            block,
        ),
        out_specs=(block, block),
        check_vma=False,
    )
```

```python
import functools

import jax
import jax.numpy as jnp
from jax import lax
from jax.experimental import pallas as pl
from jax.experimental.pallas import tpu as pltpu
from jax.sharding import PartitionSpec as P

step_dt = 0.05
wide = 6

ways = ((-1, 0), (1, 0), (0, 1), (0, -1), (-1, 1), (1, -1), (-1, -1), (1, 1))
opposite = (1, 0, 3, 2, 5, 4, 7, 6)


def roll_lanes(x, shift):
    shift = shift % x.shape[-1]
    return x if shift == 0 else pltpu.roll(x, shift, x.ndim - 1)


def roll_rows(x, shift):
    return pltpu.roll(x, shift % x.shape[-2], x.ndim - 2)


def width_of(step, width):
    return max(1, width - 1 - step % width)


def stride_of(width):
    half = 1
    while half < width:
        half *= 2
    return 2 * half


def near_rows(name):
    return 2 if isinstance(name, str) and name.startswith("adjoint") else 1


def state_groups(steps, width):
    groups = []
    for step in range(steps):
        key = (step // width, max(4, stride_of(width_of(step, width))))
        if groups and groups[-1][0] == key:
            groups[-1][1].append(step)
        else:
            groups.append((key, [step]))
    return [names for _, names in groups]


def kernel(
    width, counts, factors_at, coeffs_at, kappa_at, terminal_at, adjoint_out, gradient_out,
    factors, coeffs, kappa_in, terminal, load_sem, natural, row_send, row_recv, low_send, low_recv, pack_send, pack_recv, corner_send,
    corner_recv, send_sem, recv_sem,
):
    gx_count, gy_count, col_count = counts
    steps = coeffs.shape[0]
    ranks = factors.shape[0]
    rows = natural.shape[1] // 16
    rounds = steps // width
    group = lax.axis_index("groups")
    gx = lax.axis_index("gx")
    y = lax.axis_index("gy") * col_count + lax.axis_index("col")
    y_count = gy_count * col_count

    def inside(way):
        ok = None
        for at, move, count in ((gx, way[0], gx_count), (y, way[1], y_count)):
            if move == 0:
                continue
            here = at > 0 if move < 0 else at < count - 1
            ok = here if ok is None else jnp.logical_and(ok, here)
        return ok

    def device(way):
        far = y + way[1]
        return (group, gx + way[0], far // col_count, far % col_count)

    exists = [inside(way) for way in ways]

    loads = [
        pltpu.make_async_copy(source, target, load_sem.at[i])
        for i, (source, target) in enumerate(
            ((terminal_at, terminal), (kappa_at, kappa_in), (coeffs_at, coeffs),
             (factors_at, factors)))
    ]
    for copy_in in loads:
        copy_in.start()

    barrier = pltpu.get_barrier_semaphore()
    total = jnp.int32(0)
    for m, way in enumerate(ways):
        @pl.when(exists[m])
        def _(way=way):
            pl.semaphore_signal(
                barrier, inc=1, device_id=device(way), device_id_type=pl.DeviceIdType.MESH
            )
        total = total + exists[m].astype(jnp.int32)

    for m in range(8):
        @pl.when(jnp.logical_not(exists[m]))
        def _(m=m):
            if m < 2:
                row_recv[m] = jnp.zeros(row_recv.shape[1:], jnp.float32)
                low_recv[m] = jnp.zeros(low_recv.shape[1:], jnp.bfloat16)
            elif m < 4:
                pack_recv[m - 2] = jnp.zeros(pack_recv.shape[1:], jnp.float32)
            else:
                corner_recv[m - 4] = jnp.zeros(corner_recv.shape[1:], jnp.bfloat16)

    spans = {}
    at = low_at = 0
    group_rows = []
    low_rows = []
    lows = {}
    by_step = state_groups(steps, width)
    fields_of = [["kappa", "adjoint0"], *by_step]
    for r in range(1, rounds):
        fields_of.append(["adjoint%d" % r])
    group_of = {}
    home = {}
    tiles = 0
    group_tiles = []
    for g, names in enumerate(fields_of):
        row_start, low_start = at, low_at
        slot = 0
        for name in names:
            w = width_of(name, width) if isinstance(name, int) else width
            if name == names[0]:
                room = 128 // stride_of(w)
            spans[name] = (at, w)
            home[name] = (tiles + slot // room, slot % room)
            group_of[name] = g
            near = min(w, near_rows(name))
            lows[name] = (low_at, near)
            at += near
            low_at += w - near
            slot += rows
        group_rows.append((row_start, at - row_start))
        low_rows.append((low_start, low_at - low_start))
        count = -(-slot // room)
        group_tiles.append((tiles, count))
        tiles += count

    lane = lax.broadcasted_iota(jnp.int32, (8, 128), 1)

    def refs(g, m, to):
        if m < 2:
            span = pl.ds(*group_rows[g])
            return row_send.at[m, span], row_recv.at[to, span]
        if m >= 8:
            span = pl.ds(*low_rows[g])
            return low_send.at[m - 8, span], low_recv.at[to - 8, span]
        span = pl.ds(*group_tiles[g])
        if m < 4:
            return pack_send.at[span], pack_recv.at[to - 2, span]
        return corner_send.at[span], corner_recv.at[to - 4, span]

    def turned(m):
        return 17 - m if m >= 8 else opposite[m]

    def copy(g, m, arriving=False):
        leaves, lands = (turned(m), m) if arriving else (m, turned(m))
        source, target = refs(g, leaves, lands)
        return pltpu.make_async_remote_copy(
            src_ref=source, dst_ref=target,
            send_sem=send_sem.at[g, leaves], recv_sem=recv_sem.at[g, lands],
            device_id=device(ways[m % 8]), device_id_type=pl.DeviceIdType.MESH,
        )

    def pack(g, values):
        names = fields_of[g]
        stride = stride_of(spans[names[0]][1])
        slot_at = ((lane + stride // 2) % 128) // stride
        packed = [{}, {}]
        for name, value in zip(names, values):
            (first, w), (low_first, near) = spans[name], lows[name]
            for half in range(2):
                row_send[0, first : first + near, half] = value[half][:near]
                row_send[1, first : first + near, half] = value[half][rows - near :]
                for x in range(rows):
                    tile, slot = home[name][0], home[name][1] + x
                    moved = roll_lanes(value[half][x], slot * stride)
                    held = packed[half]
                    held[tile] = (
                        jnp.where(slot_at == slot, moved, held[tile]) if tile in held else moved)
            if w > near:
                both = jnp.concatenate(value, axis=1).astype(jnp.bfloat16)
                low_send[0, low_first : low_first + w - near] = both[near:w]
                low_send[1, low_first : low_first + w - near] = both[rows - w : rows - near]
        for tile in packed[0]:
            pack_send[tile, 0] = packed[0][tile]
            pack_send[tile, 1] = packed[1][tile]
            both = jnp.concatenate([packed[0][tile], packed[1][tile]], axis=0)
            corner_send[tile] = both.astype(jnp.bfloat16)

    def used(g):
        corners = any(spans[name][1] > 1 for name in fields_of[g])
        messages = list(range(2))
        if low_rows[g][1]:
            messages += [8, 9]
        return list(range(4, 8 if corners else 4)) + messages + [2, 3]

    def send(g):
        for m in used(g):
            @pl.when(exists[m % 8])
            def _(m=m):
                copy(g, m).start()

    def arrive(g):
        for m in used(g):
            @pl.when(exists[m % 8])
            def _(m=m):
                copy(g, m, arriving=True).wait_recv()

    def padded(name, value):
        g, (tile_at, base) = group_of[name], home[name]
        first, w = spans[name]
        stride = stride_of(spans[fields_of[g][0]][1])
        from_right = lane % stride < stride // 2
        low_first, near = lows[name]
        center, halo = [], []
        outer = [[], []]
        if w > near:
            outer = [
                [low_recv[side, low_first : low_first + w - near].astype(jnp.float32)]
                for side in range(2)
            ]

        def corner(way, half):
            return corner_recv[way - 4, tile_at].astype(jnp.float32)[8 * half : 8 * half + 8]

        for half in range(2):
            part = slice(8 * half, 8 * half + 8)
            center.append(jnp.concatenate(
                [*(x[:, part] for x in outer[0]), row_recv[0, first : first + near, half],
                 value[half], row_recv[1, first : first + near, half],
                 *(x[:, part] for x in outer[1])], axis=0))
            own = jnp.where(from_right, pack_recv[0, tile_at, half], pack_recv[1, tile_at, half])
            parts = [(own, range(rows))]
            if w > 1:
                up = jnp.where(from_right, corner(4, half), corner(6, half))
                down = jnp.where(from_right, corner(7, half), corner(5, half))
                parts = [(up, range(rows - w + 1, rows)), *parts, (down, range(w - 1))]
            halo.append(jnp.stack(
                [roll_lanes(tile, -(base + x) * stride) for tile, at in parts for x in at]))
        return center, halo

    def load(ref):
        return [
            jnp.stack([ref[pl.ds(half * rows + x, 8, stride=2 * rows), :] for x in range(rows)])
            for half in range(2)
        ]

    def trim(x, extra):
        return x[extra : x.shape[0] - extra] if extra else x

    loads[0].wait()
    adjoint = load(terminal)
    loads[1].wait()
    kappa = [x * (0.5 * step_dt) for x in load(kappa_in)]
    pack(0, [kappa, adjoint])
    pl.semaphore_wait(barrier, total)
    send(0)

    loads[2].wait()
    loads[3].wait()
    states = []
    factor = [factors[k].astype(jnp.float32) for k in range(ranks)]
    for at_group, names in enumerate(by_step):
        for index in names:
            t = steps - 1 - index
            total_state = coeffs[t, 0] * factor[0]
            for k in range(1, ranks):
                total_state = total_state + coeffs[t, k] * factor[k]
            natural[index] = total_state.reshape(natural.shape[1:])
            states.append(load(natural.at[index]))
        pack(1 + at_group, [states[index] for index in names])
        send(1 + at_group)

    last = lane == 127
    start_lane = lane == 0
    near = lane < 64
    lane_ok = jnp.logical_or(
        jnp.logical_and(near, exists[2]), jnp.logical_and(jnp.logical_not(near), exists[3]))

    def ahead(center, halo):
        c, h = roll_lanes(center, -1), roll_lanes(halo, -1)
        return jnp.where(last, h, c), jnp.where(last, c, h)

    def behind(center, halo):
        c, h = roll_lanes(center, 1), roll_lanes(halo, 1)
        return jnp.where(start_lane, h, c), jnp.where(start_lane, c, h)

    def masked(x, b):
        if b == 0:
            return x
        return jnp.concatenate(
            [jnp.where(exists[0], x[:b], 0.0), x[b : b + rows],
             jnp.where(exists[1], x[b + rows :], 0.0)], axis=0)

    arrive(0)
    kc, kh = padded("kappa", kappa)
    face_x = [[x[half][1:] + x[half][:-1] for half in range(2)] for x in (kc, kh)]
    face_y = []
    for half in range(2):
        c = trim(kc[half], 1)
        ca, ha = ahead(c, kh[half])
        face_y.append((c + ca, kh[half] + ha))
    face_z = [(x[0] + x[1], x[1] + roll_rows(x[0], -1)) for x in (kc, kh)]

    gradient = [jnp.zeros((rows, 8, 128), jnp.float32) for _ in range(2)]
    for r in range(rounds):
        if r:
            pack(len(by_step) + r, [adjoint])
            send(len(by_step) + r)
            arrive(len(by_step) + r)
        vc, vh = padded("adjoint%d" % r, adjoint)
        for j in range(width):
            index = r * width + j
            if index == fields_of[group_of[index]][0]:
                arrive(group_of[index])
            a = width - j
            b = a - 1
            skip = width - a
            sc, sh = padded(index, states[index])
            sw = spans[index][1]
            new_c, new_h = [None, None], [None, None]
            for half in range(2):
                d = vc[half][1:] - vc[half][:-1]
                flux = trim(face_x[0][half], skip) * d
                new_c[half] = flux[1:] - flux[:-1]
                ds = trim(sc[half], sw - 1)
                product = (ds[1:] - ds[:-1]) * trim(d, b)
                gradient[half] = gradient[half] + (product[1:] + product[:-1])
                if b:
                    d = vh[half][1:] - vh[half][:-1]
                    flux = trim(face_x[1][half], skip) * d
                    new_h[half] = flux[1:] - flux[:-1]
            for half in range(2):
                c, h = trim(vc[half], 1), vh[half]
                ca, ha = ahead(c, h)
                dc, dh = ca - c, ha - h
                fc = trim(face_y[half][0], skip) * dc
                fh = trim(face_y[half][1], skip) * dh
                bc, bh = behind(fc, fh)
                new_c[half] = new_c[half] + (fc - bc)
                if b:
                    new_h[half] = new_h[half] + trim(fh - bh, 1)
                c, h = trim(sc[half], sw), trim(sh[half], sw - 1)
                ca, ha = ahead(c, h)
                pc = (ca - c) * trim(dc, b)
                ph = (ha - h) * trim(dh, b)
                bc, _ = behind(pc, ph)
                gradient[half] = gradient[half] + (pc + bc)
            for which, v, new, extra in ((0, vc, new_c, skip + 1), (1, vh, new_h, skip + 1)):
                if which and not b:
                    continue
                v0, v1 = trim(v[0], 1), trim(v[1], 1)
                inner, outer = v1 - v0, roll_rows(v0, -1) - v1
                fi = trim(face_z[which][0], extra) * inner
                fo = trim(face_z[which][1], extra) * outer
                new[0] = new[0] + (fi - roll_rows(fo, 1))
                new[1] = new[1] + (fo - fi)
                if not which:
                    s0, s1 = trim(sc[0], sw), trim(sc[1], sw)
                    pi = (s1 - s0) * trim(inner, b)
                    po = (roll_rows(s0, -1) - s1) * trim(outer, b)
                    gradient[0] = gradient[0] + (pi + roll_rows(po, 1))
                    gradient[1] = gradient[1] + (pi + po)
            for half in range(2):
                s = trim(sc[half], sw - b)
                v = trim(vc[half], 1)
                new_c[half] = masked(
                    v * ((1.0 + step_dt) - (3.0 * step_dt) * s * s) + new_c[half], b)
                if b:
                    s = trim(sh[half], sw - b)
                    v = trim(vh[half], 1)
                    moved = v * ((1.0 + step_dt) - (3.0 * step_dt) * s * s) + new_h[half]
                    new_h[half] = jnp.where(lane_ok, masked(moved, b - 1), 0.0)
            vc, vh = new_c, new_h
        adjoint = vc

    for half in range(2):
        for x in range(rows):
            where = pl.ds(half * rows + x, 8, stride=2 * rows)
            adjoint_out[where, :] = adjoint[half][x]
            gradient_out[where, :] = gradient[half][x] * (-0.5 * step_dt)

    for g in range(len(fields_of)):
        for m in used(g):
            @pl.when(exists[m % 8])
            def _(g=g, m=m):
                copy(g, m).wait_send()


def store(adjoint, gradient, adjoint_out, gradient_out, sem):
    copies = [
        pltpu.make_async_copy(adjoint, adjoint_out, sem.at[0]),
        pltpu.make_async_copy(gradient, gradient_out, sem.at[1]),
    ]
    for copy in copies:
        copy.start()
    for copy in copies:
        copy.wait()


def per_device(counts, factors, coeffs, diffusivity, terminal):
    thick, rows, lanes = terminal.shape
    steps = coeffs.shape[0]
    width = wide
    rounds = steps // width
    by_step = state_groups(steps, width)
    groups = len(by_step) + rounds
    tiles = 2 * groups
    fields = ["kappa", *("adjoint%d" % r for r in range(rounds)), *range(steps)]
    widths = [width if isinstance(name, str) else width_of(name, width) for name in fields]
    near = sum(min(w, near_rows(name)) for w, name in zip(widths, fields))
    far = max(1, sum(widths) - near)
    flat = (thick * rows, lanes)
    vmem = pl.BlockSpec(memory_space=pltpu.VMEM)
    adjoint, gradient = pl.pallas_call(
        functools.partial(kernel, width, counts),
        out_shape=[jax.ShapeDtypeStruct(flat, jnp.float32)] * 2,
        in_specs=[pl.BlockSpec(memory_space=pltpu.HBM)] * 4,
        out_specs=[vmem, vmem],
        scratch_shapes=[
            pltpu.VMEM(factors.shape, factors.dtype),
            pltpu.SMEM(coeffs.shape, jnp.float32),
            pltpu.VMEM(flat, jnp.float32),
            pltpu.VMEM(flat, jnp.float32),
            pltpu.SemaphoreType.DMA((4,)),
            pltpu.VMEM((steps, *flat), jnp.float32),
            pltpu.VMEM((2, near, 2, 8, lanes), jnp.float32),
            pltpu.VMEM((2, near, 2, 8, lanes), jnp.float32),
            pltpu.VMEM((2, far, 16, lanes), jnp.bfloat16),
            pltpu.VMEM((2, far, 16, lanes), jnp.bfloat16),
            pltpu.VMEM((tiles, 2, 8, lanes), jnp.float32),
            pltpu.VMEM((2, tiles, 2, 8, lanes), jnp.float32),
            pltpu.VMEM((tiles, 16, lanes), jnp.bfloat16),
            pltpu.VMEM((4, tiles, 16, lanes), jnp.bfloat16),
            pltpu.SemaphoreType.DMA((groups, 10)),
            pltpu.SemaphoreType.DMA((groups, 10)),
        ],
        compiler_params=pltpu.CompilerParams(
            collective_id=0, has_side_effects=True, vmem_limit_bytes=60 * 1024 * 1024
        ),
    )(factors, coeffs, diffusivity.reshape(flat), terminal.reshape(flat))
    adjoint, gradient = pl.pallas_call(
        store,
        out_shape=[jax.ShapeDtypeStruct(flat, jnp.float32)] * 2,
        in_specs=[vmem] * 2,
        out_specs=[pl.BlockSpec(memory_space=pltpu.HBM)] * 2,
        scratch_shapes=[pltpu.SemaphoreType.DMA((2,))],
    )(adjoint, gradient)
    return adjoint.reshape(terminal.shape), gradient.reshape(terminal.shape)


def solution(mesh):
    block = P(None, ("groups", "gx"), ("gy", "col"))
    counts = (mesh.shape["gx"], mesh.shape["gy"], mesh.shape["col"])
    return jax.shard_map(
        functools.partial(per_device, counts),
        mesh=mesh,
        in_specs=(
            P(None, None, ("groups", "gx"), ("gy", "col")),
            P("groups", None),
            block,
            block,
        ),
        out_specs=(block, block),
        check_vma=False,
    )
```
